256 devices in a mesh: amp: 32 (over y, z), ints: 8 (over x, core).
Axes of the slice: x: 4, y: 4, z: 8, core: 2. Of those that a mesh axis runs over, the one named last changes fastest.
Arguments:
- amplitudes: bfloat16 [64, 1024, 1024], P('amp', None, 'ints'), may hold values from -6 to 6
- fock_vv: bfloat16 [1024, 1024], replicated, may hold values from -0.1875 to 0.1875
- cycle_ints: bfloat16 [4, 1024, 4, 1024], P(None, 'amp', None, 'ints'), may hold values from -0.15625 to 0.15625
- tile_mask: int32 [16, 16], replicated, may hold values 0 or 1
Outputs:
- residual: bfloat16 [64, 1024, 1024], P('amp', None, 'ints')
The draws below stay inside these ranges and needn't reach their ends.
All inputs are finite; a program needn't handle non-finite values.
Results may differ from the reference program's by a relative error of at most 0.0034.
Values may be sent and summed in bfloat16 or wider, within the bound.
No kernel may reach another device: no remote copies, remote signals or barrier semaphores. Data moves between devices by JAX's collectives and lax.ppermute only.
A program may use at most 64 MiB of HBM per device.

```python
import jax
import jax.numpy as jnp
from jax import lax

VB = 64
NVB = 16
NO = 4
NI = 16
V = 1024
NP = 64


def touch_ends(entries, rng, least, largest):
    spot = [jax.random.randint(jax.random.fold_in(rng, axis), (), 0, length) for axis, length in enumerate(entries.shape)]
    longest = entries.shape.index(max(entries.shape))
    neighbour = spot[:longest] + [(spot[longest] + 1) % entries.shape[longest]] + spot[longest + 1:]
    return entries.at[tuple(spot)].set(least).at[tuple(neighbour)].set(largest)


def level_of(rng, extent, cuts, smallest, high):
    def one(position, shards_of):
        draws = jax.random.uniform(jax.random.fold_in(jax.random.fold_in(rng, 6), position), (shards_of,), jnp.float32, smallest / len(cuts), high / len(cuts))
        return jnp.repeat(jnp.exp(draws), extent[position] // shards_of).reshape((-1,) + (1,) * (len(extent) - position - 1))

    factor_of = one(*cuts[0])
    for cut in cuts[1:]:
        factor_of = factor_of * one(*cut)
    return factor_of


def normal_values(own_key, shape, width, limit, shards=(), held_as=jnp.bfloat16):
    loudness = level_of(own_key, shape, shards, -0.22, 0.18) if shards else 1.0
    values = jax.random.normal(own_key, shape, jnp.float32) * width * loudness
    return jnp.minimum(jnp.maximum(values, -limit), limit).astype(held_as)


def setup_inputs(seed: int = 0) -> dict:
    keys = jax.random.split(jax.random.key(seed), 5)
    return {
        "amplitudes": normal_values(keys[0], (NP, V, V), 1.0, 6.0, ((0, 32), (2, 8))),
        "fock_vv": normal_values(keys[1], (V, V), V ** -0.5, 0.1875),
        "cycle_ints": normal_values(keys[2], (NO, V, NO, V), (NO * V * 3 // 10) ** -0.5, 0.15625, ((1, 32), (3, 8))),
        "tile_mask": touch_ends((jax.random.randint(keys[3], (NVB, NVB), 0, 10) < 3).astype(jnp.int32), jax.random.fold_in(keys[3], 1), 0, 1),
    }


def reference(amplitudes, fock_vv, cycle_ints, tile_mask):
    block_ids = jnp.arange(V) // VB
    expanded = tile_mask[block_ids[:, None], block_ids[None, :]]
    masked = cycle_ints * expanded.astype(jnp.bfloat16)[None, :, None, :]
    amps_f = amplitudes.astype(jnp.float32)
    fock_f = fock_vv.astype(jnp.float32)
    left_term = jnp.einsum("ac,pcb->pab", fock_f, amps_f)
    right_term = jnp.einsum("pac,bc->pab", amps_f, fock_f)
    grouped = amplitudes.reshape(NI, NO, V, V)
    matrix = masked.reshape(NO * V, NO * V)

    def cycle_row(slab_amps):
        rows = jnp.transpose(slab_amps, (1, 0, 2)).reshape(V, NO * V)
        product = jnp.dot(rows, matrix, preferred_element_type=jnp.float32)
        return jnp.transpose(product.reshape(V, NO, V), (1, 0, 2)).astype(jnp.bfloat16)

    cycle_term = lax.map(cycle_row, grouped).reshape(NP, V, V)
    total = left_term + right_term + cycle_term.astype(jnp.float32)
    return total.astype(jnp.bfloat16)
```

```python
import jax
import jax.numpy as jnp
from jax import lax
from jax.experimental import pallas as pl
from jax.experimental.pallas import tpu as pltpu
from jax.sharding import PartitionSpec as P

NX, NY, NZ = 4, 4, 8
X_RING = lambda d: [(2 * x + c, 2 * ((x + d) % NX) + c) for x in range(NX) for c in range(2)]
Y_RING = lambda d: [(y * NZ + z, ((y + d) % NY) * NZ + z) for y in range(NY) for z in range(NZ)]
Z_PAIR = [(p, p ^ 1) for p in range(NY * NZ)]
CORES = [(q, q ^ 1) for q in range(2 * NX)]
Z_GROUPS = [[y * NZ + z for z in range(NZ)] for y in range(NY)]
ROWS = 256
MIB = 1 << 20


def fock_kernel(at_ref, fock_ref, rows_ref, amps_ref, *refs):
    mine, swapped, out_ref = refs[:NX], refs[NX : 2 * NX], refs[2 * NX]
    x, core = at_ref[2], at_ref[3]
    both = jnp.concatenate([amps_ref[0], amps_ref[1]], axis=1)
    left = jnp.dot(fock_ref[...], both, preferred_element_type=jnp.float32)
    width = amps_ref.shape[2]
    fock = []
    for d in range(NX):
        for c in (core, 1 - core):
            start = pl.multiple_of((2 * lax.rem(x + d, NX) + c) * width, width)
            fock.append(rows_ref[:, pl.ds(start, width)])
    fock = jnp.concatenate(fock, axis=1)
    for p in range(2):
        rows = jnp.concatenate([r[p] for d in range(NX) for r in (mine[d], swapped[d])], axis=1)
        right = lax.dot_general(
            rows, fock, (((1,), (1,)), ((), ())), preferred_element_type=jnp.float32
        )
        out_ref[p] = left[:, p * width : (p + 1) * width] + right


def fock_terms(at, fock_vv, amplitudes, mine, swapped):
    pairs, width, cols = amplitudes.shape
    block = pl.BlockSpec((pairs, ROWS, cols), lambda r, at: (0, r, 0))
    return pl.pallas_call(
        fock_kernel,
        out_shape=jax.ShapeDtypeStruct((pairs, width, cols), jnp.float32),
        grid_spec=pltpu.PrefetchScalarGridSpec(
            num_scalar_prefetch=1,
            grid=(width // ROWS,),
            in_specs=[
                pl.BlockSpec((ROWS, width), lambda r, at: (r, 0)),
                pl.BlockSpec((cols, width), lambda r, at: (2 * at[2] + at[3], 0)),
                pl.BlockSpec((pairs, width, cols), lambda r, at: (0, 0, 0)),
            ]
            + [block] * (2 * NX),
            out_specs=block,
        ),
        compiler_params=pltpu.CompilerParams(vmem_limit_bytes=24 * MIB),
        cost_estimate=pl.CostEstimate(
            flops=2 * pairs * width * width * cols * 2, bytes_accessed=9 * MIB, transcendentals=0
        ),
    )(at, fock_vv, fock_vv, amplitudes, *mine, *swapped)


def cycle_kernel(at_ref, fock_ref, *refs):
    amps, ints, out_ref, held = refs[: 4 * NX], refs[4 * NX : 4 * NX + NY], refs[-2], refs[-1]
    y, half, x, core = at_ref[0], lax.rem(at_ref[1], 2), at_ref[2], at_ref[3]

    @pl.when(pl.program_id(0) == 0)
    def _():
        for e in range(NY):
            held[lax.rem(y + e, NY)] = ints[e][...]

    n_z, _, depth, cols = ints[0].shape[0:4]
    side = n_z // 2
    total = None
    for d in range(NX):
        lhs, rhs = [], []
        for o in range(2):
            mine, swapped = amps[2 * NX * o + d], amps[2 * NX * o + NX + d]
            for p in range(2):
                k = 2 * (half if o == 0 else 1 - half) + p
                for ref, c in ((mine, core), (swapped, 1 - core)):
                    lhs.append(ref[p])
                    part = held[lax.rem(x + d, NX), pl.ds(c * side, side), k]
                    rhs.append(part.reshape(side * depth, cols))
        term = jnp.dot(
            jnp.concatenate(lhs, axis=1),
            jnp.concatenate(rhs, axis=0),
            preferred_element_type=jnp.float32,
        )
        total = term if total is None else total + term
    width = cols // 2
    total = total.astype(jnp.bfloat16).astype(jnp.float32)
    for p in range(2):
        out_ref[p] = (fock_ref[p] + total[:, p * width : (p + 1) * width]).astype(jnp.bfloat16)


def cycle_sum(at, fock_part, amps, ints):
    pairs, width, cols = fock_part.shape
    block = pl.BlockSpec((pairs, ROWS, cols), lambda r, at: (0, r, 0))
    whole = pl.BlockSpec(ints[0].shape, lambda r, at: (0, 0, 0, 0))
    return pl.pallas_call(
        cycle_kernel,
        out_shape=jax.ShapeDtypeStruct((pairs, width, cols), jnp.bfloat16),
        grid_spec=pltpu.PrefetchScalarGridSpec(
            num_scalar_prefetch=1,
            grid=(width // ROWS,),
            in_specs=[block] * (1 + 4 * NX) + [whole] * NY,
            out_specs=block,
            scratch_shapes=[pltpu.VMEM((NY,) + ints[0].shape, jnp.bfloat16)],
        ),
        compiler_params=pltpu.CompilerParams(vmem_limit_bytes=32 * MIB),
        cost_estimate=pl.CostEstimate(
            flops=2 * width * 4 * width * pairs * cols, bytes_accessed=12 * MIB, transcendentals=0
        ),
    )(at, fock_part, *amps, *ints)


def body(amplitudes, fock_vv, cycle_ints, tile_mask):
    amp, ints = lax.axis_index("amp"), lax.axis_index("ints")
    at = jnp.stack([amp // NZ, amp % NZ, ints // 2, ints % 2]).astype(jnp.int32)
    occ, depth, _, cols = cycle_ints.shape
    block = fock_vv.shape[0] // tile_mask.shape[0]

    present = lax.dynamic_slice(
        tile_mask, (amp * depth // block, ints * cols // block), (1, cols // block)
    )
    present = jnp.repeat(present[0].astype(jnp.bfloat16), block)
    masked = cycle_ints * present
    halves = masked.reshape(occ, depth, 2, 2 * cols).transpose(2, 0, 1, 3)
    to_z = jnp.broadcast_to(halves[None], (NZ // 2,) + halves.shape)
    to_z = to_z.reshape((NZ,) + halves.shape[1:])
    row = lax.all_to_all(to_z, "amp", 0, 0, tiled=True, axis_index_groups=Z_GROUPS)
    ints_by_y = [row] + [lax.ppermute(row, "amp", Y_RING(-e)) for e in (1, 2, 3)]

    own = [amplitudes] + [lax.ppermute(amplitudes, "ints", X_RING(-d)) for d in (1, 2, 3)]
    partner = lax.ppermute(amplitudes, "amp", Z_PAIR)
    other = [
        partner,
        lax.ppermute(partner, "ints", X_RING(-1)),
        lax.ppermute(own[2], "amp", Z_PAIR),
        lax.ppermute(partner, "ints", X_RING(-3)),
    ]
    own_swapped = [lax.ppermute(t, "ints", CORES) for t in own]
    other_swapped = [lax.ppermute(t, "ints", CORES) for t in other]

    fock_part = fock_terms(at, fock_vv, amplitudes, own, own_swapped)
    return cycle_sum(at, fock_part, own + own_swapped + other + other_swapped, ints_by_y)


def solution(mesh):
    in_specs = (P("amp", None, "ints"), P(), P(None, "amp", None, "ints"), P())
    out_specs = P("amp", None, "ints")
    return jax.shard_map(body, mesh=mesh, in_specs=in_specs, out_specs=out_specs, check_vma=False)
```

```python
import functools

import jax
import jax.numpy as jnp
from jax import lax
from jax.experimental import pallas as pl
from jax.experimental.pallas import tpu as pltpu
from jax.sharding import PartitionSpec as P

NX, NY, NZ = 4, 4, 8
X_RING = lambda d: [(2 * x + c, 2 * ((x + d) % NX) + c) for x in range(NX) for c in range(2)]
Y_RING = lambda d: [(y * NZ + z, ((y + d) % NY) * NZ + z) for y in range(NY) for z in range(NZ)]
Z_PAIR = [(p, p ^ 1) for p in range(NY * NZ)]
CORES = [(q, q ^ 1) for q in range(2 * NX)]
X_GROUPS = [[2 * x + c for x in range(NX)] for c in range(2)]
Y_GROUPS = [[y * NZ + z for y in range(NY)] for z in range(NZ)]
Z_GROUPS = [[y * NZ + z for z in range(NZ)] for y in range(NY)]
ROWS = 256
MIB = 1 << 20


VM = 16
COST = 1


VMEM = pl.BlockSpec(memory_space=pltpu.VMEM)
SMEM = pl.BlockSpec(memory_space=pltpu.SMEM)


def fock_kernel(at_ref, fock_ref, rows_ref, *refs):
    amps, out_ref = refs[:-1], refs[-1]
    x, core = at_ref[2], at_ref[3]
    own = amps[0]
    width = own.shape[2]
    both = jnp.concatenate([own[0], own[1]], axis=1)
    fock = []
    for i in range(len(amps)):
        chip, c = lax.rem(x + i // 2, NX), (1 - core if i % 2 else core)
        start = pl.multiple_of((2 * chip + c) * width, width)
        fock.append(rows_ref[:, pl.ds(start, width)])
    fock = jnp.concatenate(fock, axis=1)

    @pl.loop(0, fock_ref.shape[0] // ROWS)
    def _(r):
        at = pl.ds(pl.multiple_of(r * ROWS, ROWS), ROWS)
        left = jnp.dot(fock_ref[at, :], both, preferred_element_type=jnp.float32)
        for p in range(2):
            rows = jnp.concatenate([a[p, at, :] for a in amps], axis=1)
            right = lax.dot_general(
                rows, fock, (((1,), (1,)), ((), ())), preferred_element_type=jnp.float32
            )
            out_ref[p, at, :] = left[:, p * width : (p + 1) * width] + right


def fock_terms(at, fock_vv, fock_rows, amps):
    pairs, width, cols = amps[0].shape
    return pl.pallas_call(
        fock_kernel,
        out_shape=jax.ShapeDtypeStruct((pairs, width, cols), jnp.float32),
        in_specs=[SMEM] + [VMEM] * (2 + len(amps)),
        out_specs=VMEM,
        compiler_params=pltpu.CompilerParams(vmem_limit_bytes=VM * MIB),
        cost_estimate=pl.CostEstimate(
            flops=2 * pairs * width * width * cols * 2, bytes_accessed=4 * MIB, transcendentals=0
        ),
    )(at, fock_vv, fock_rows, *amps)


def cycle_kernel(last, at_ref, *refs):
    fock_ref = sent_ref = None
    if last:
        fock_ref, sent_ref, refs = refs[0], refs[1], refs[2:]
    held, out_ref, refs = refs[-1], refs[-2], refs[:-2]
    ints, amps = refs[-NY:], refs[:-NY]
    y, x, core = at_ref[0], at_ref[2], at_ref[3]
    n_z, pairs, depth, cols = ints[0].shape
    side, width = n_z // 2, cols // 2
    for e in range(NY):
        d = lax.rem(y + e - x + 2 * NX, NX)
        for s in range(2):
            c = 1 - core if s else core
            for p in range(pairs):
                part = ints[e][pl.ds(c * side, side), p]
                held[d, s, p] = part.reshape(side * depth, cols)
    rhs = jnp.concatenate(
        [held[i // 2, i % 2, p] for p in range(pairs) for i in range(len(amps))], axis=0
    )

    @pl.loop(0, out_ref.shape[1] // ROWS)
    def _(r):
        at = pl.ds(pl.multiple_of(r * ROWS, ROWS), ROWS)
        lhs = jnp.concatenate([a[p, at, :] for p in range(pairs) for a in amps], axis=1)
        total = jnp.dot(lhs, rhs, preferred_element_type=jnp.float32)
        for p in range(pairs):
            mine_p = total[:, p * width : (p + 1) * width]
            if last:
                mine_p = mine_p + sent_ref[p, at, :].astype(jnp.float32)
                mine_p = mine_p.astype(jnp.bfloat16).astype(jnp.float32) + fock_ref[p, at, :]
            out_ref[p, at, :] = mine_p.astype(out_ref.dtype)


def cycle_sum(at, before, amps, ints, shape, cost):
    n_z, pairs, depth, cols = ints[0].shape
    last = bool(before)
    return pl.pallas_call(
        functools.partial(cycle_kernel, last),
        out_shape=jax.ShapeDtypeStruct(shape, jnp.bfloat16),
        in_specs=[SMEM] + [VMEM] * (len(before) + len(amps) + len(ints)),
        out_specs=VMEM,
        scratch_shapes=[pltpu.VMEM((NY, 2, pairs, n_z // 2 * depth, cols), jnp.bfloat16)],
        compiler_params=pltpu.CompilerParams(vmem_limit_bytes=VM * MIB),
        cost_estimate=pl.CostEstimate(
            flops=cost * shape[0] * shape[1] * shape[1] * shape[2] * 4,
            bytes_accessed=6 * MIB,
            transcendentals=0,
        ),
    )(at, *before, *amps, *ints)


def prepare_kernel(at_ref, mask_ref, ints_ref, out_ref):
    occ, depth, n_j, cols = ints_ref.shape
    block = n_j * NZ * NY * depth // n_j // mask_ref.shape[0]
    amp, q = at_ref[0] * NZ + at_ref[1], 2 * at_ref[2] + at_ref[3]
    place = lax.broadcasted_iota(jnp.int32, (depth, cols), 1) // block
    keep = jnp.zeros((depth, cols), jnp.float32)
    for b in range(cols // block):
        present = mask_ref[amp * depth // block, q * (cols // block) + b].astype(jnp.float32)
        keep = jnp.where(place == b, present, keep)
    keep = keep.astype(jnp.bfloat16)
    for k in range(occ):
        for j in range(2):
            pair = [ints_ref[k, :, 2 * j + p, :] * keep for p in range(2)]
            pair = jnp.concatenate(pair, axis=1)
            part = int(j == k // 2)
            for z in range(k // 2, NZ, 2):
                out_ref[part, z, k % 2] = pair


def prepare(at, tile_mask, cycle_ints):
    occ, depth, _, cols = cycle_ints.shape
    shape = (2, NZ, occ // 2, depth, 2 * cols)
    return pl.pallas_call(
        prepare_kernel,
        out_shape=jax.ShapeDtypeStruct(shape, jnp.bfloat16),
        grid_spec=pltpu.PrefetchScalarGridSpec(
            num_scalar_prefetch=2,
            grid=(1,),
            in_specs=[pl.BlockSpec(cycle_ints.shape, lambda r, at, mask: (0, 0, 0, 0))],
            out_specs=pl.BlockSpec(shape, lambda r, at, mask: (0, 0, 0, 0, 0)),
        ),
        compiler_params=pltpu.CompilerParams(vmem_limit_bytes=16 * MIB),
    )(at, tile_mask, cycle_ints)


def swap(a):
    return lax.ppermute(a, "ints", CORES)


def along_z(a):
    return lax.all_to_all(a, "amp", 0, 0, tiled=True, axis_index_groups=Z_GROUPS)


def along_y(row):
    return [row] + [lax.ppermute(row, "amp", Y_RING(-e)) for e in (1, 2, 3)]


def body(amplitudes, fock_vv, cycle_ints, tile_mask):
    amp, ints = lax.axis_index("amp"), lax.axis_index("ints")
    at = jnp.stack([amp // NZ, amp % NZ, ints // 2, ints % 2]).astype(jnp.int32)
    to_z = prepare(at, tile_mask, cycle_ints)
    rows = [along_z(to_z[0]), along_z(to_z[1])]
    partners, mine = along_y(rows[0]), along_y(rows[1])
    own = [amplitudes] + [lax.ppermute(amplitudes, "ints", X_RING(-d)) for d in (1, 2, 3)]
    own = [b for a in own for b in (a, swap(a))]

    fock_rows = lax.dynamic_slice_in_dim(fock_vv, ints * amplitudes.shape[2], amplitudes.shape[2], 0)
    fock_part = fock_terms(at, fock_vv, fock_rows, own)
    sent = cycle_sum(at, [], own, partners, amplitudes.shape, COST)
    sent = lax.ppermute(sent, "amp", Z_PAIR)
    return cycle_sum(at, [fock_part, sent], own, mine, amplitudes.shape, 1)


def solution(mesh):
    in_specs = (P("amp", None, "ints"), P(), P(None, "amp", None, "ints"), P())
    out_specs = P("amp", None, "ints")
    return jax.shard_map(body, mesh=mesh, in_specs=in_specs, out_specs=out_specs, check_vma=False)
```

```python
import functools

import jax
import jax.numpy as jnp
from jax import lax
from jax.experimental import pallas as pl
from jax.experimental.pallas import tpu as pltpu
from jax.sharding import PartitionSpec as P

NX, NY, NZ = 4, 4, 8
X_RING = lambda d: [(2 * x + c, 2 * ((x + d) % NX) + c) for x in range(NX) for c in range(2)]
Y_RING = lambda d: [(y * NZ + z, ((y + d) % NY) * NZ + z) for y in range(NY) for z in range(NZ)]
Z_PAIR = [(p, p ^ 1) for p in range(NY * NZ)]
CORES = [(q, q ^ 1) for q in range(2 * NX)]
X_GROUPS = [[2 * x + c for x in range(NX)] for c in range(2)]
Y_GROUPS = [[y * NZ + z for y in range(NY)] for z in range(NZ)]
Z_RING = lambda d: [(y * NZ + z, y * NZ + (z + d) % NZ) for y in range(NY) for z in range(NZ)]
ROWS = 256
MIB = 1 << 20


VM = 16
COST = 8
CROWS = 1024
CHUNKS = 4
MINE_COST = 8


VMEM = pl.BlockSpec(memory_space=pltpu.VMEM)
SMEM = pl.BlockSpec(memory_space=pltpu.SMEM)


def blocks_of(refs):
    return [ref.at[d] for d in range(NX) for ref in refs]


def fock_kernel(at_ref, fock_ref, rows_ref, *refs):
    amps, out_ref = refs[:-1], refs[-1]
    x, core = 0, at_ref[3]
    own, amps = amps[0], blocks_of(amps[1:])
    width = own.shape[2]
    both = jnp.concatenate([own[0], own[1]], axis=1)
    fock = []
    for i in range(len(amps)):
        chip, c = lax.rem(x + i // 2, NX), (1 - core if i % 2 else core)
        start = pl.multiple_of((2 * chip + c) * width, width)
        fock.append(rows_ref[:, pl.ds(start, width)])
    fock = jnp.concatenate(fock, axis=1)

    @pl.loop(0, fock_ref.shape[0] // ROWS)
    def _(r):
        at = pl.ds(pl.multiple_of(r * ROWS, ROWS), ROWS)
        left = jnp.dot(fock_ref[at, :], both, preferred_element_type=jnp.float32)
        for p in range(2):
            rows = jnp.concatenate([a[p, at, :] for a in amps], axis=1)
            right = lax.dot_general(
                rows, fock, (((1,), (1,)), ((), ())), preferred_element_type=jnp.float32
            )
            out_ref[p, at, :] = left[:, p * width : (p + 1) * width] + right


def fock_terms(at, fock_vv, fock_rows, amps):
    pairs, width, cols = amps[0].shape
    return pl.pallas_call(
        fock_kernel,
        out_shape=jax.ShapeDtypeStruct((pairs, width, cols), jnp.float32),
        in_specs=[SMEM] + [VMEM] * (2 + len(amps)),
        out_specs=VMEM,
        compiler_params=pltpu.CompilerParams(vmem_limit_bytes=VM * MIB),
        cost_estimate=pl.CostEstimate(
            flops=1 * 4 * pairs * width * width * cols, bytes_accessed=4 * MIB, transcendentals=0
        ),
    )(at, fock_vv, fock_rows, *amps)


def cycle_kernel(at_ref, *refs):
    held, out_ref, refs = refs[-1], refs[-2], refs[:-2]
    ints, amps = refs[-NY:], refs[:-NY]
    y, z, core = at_ref[0], at_ref[1], at_ref[3]
    amps = blocks_of(amps)
    n_z, pairs, depth, cols = ints[0].shape
    width = cols // 2
    for e in range(NY):
        chip = lax.rem(y + e, NY)
        for g in range(n_z // 2):
            place = lax.rem(z // 2 + g, n_z // 2)
            s = lax.rem(place // 2 + core, 2)
            for p in range(pairs):
                part = ints[e][2 * g : 2 * g + 2, p]
                held[chip, s, p, lax.rem(place, 2)] = part.reshape(2 * depth, cols)
    rhs = jnp.concatenate(
        [held[i // 2, i % 2, p].reshape(n_z // 2 * depth, cols) for p in range(pairs) for i in range(len(amps))], axis=0
    )

    @pl.loop(0, out_ref.shape[1] // CROWS)
    def _(r):
        at = pl.ds(pl.multiple_of(r * CROWS, CROWS), CROWS)
        lhs = jnp.concatenate([a[p, at, :] for p in range(pairs) for a in amps], axis=1)
        total = jnp.dot(lhs, rhs, preferred_element_type=jnp.float32)
        for p in range(pairs):
            out_ref[p, at, :] = total[:, p * width : (p + 1) * width].astype(out_ref.dtype)


def cycle_sum(at, amps, ints, dtype, cost):
    n_z, pairs, depth, cols = ints[0].shape
    shape = amps[0].shape[1:]
    return pl.pallas_call(
        cycle_kernel,
        out_shape=jax.ShapeDtypeStruct(shape, dtype),
        in_specs=[SMEM] + [VMEM] * (len(amps) + len(ints)),
        out_specs=VMEM,
        scratch_shapes=[pltpu.VMEM((NY, 2, pairs, 2, 2 * depth, cols), jnp.bfloat16)],
        compiler_params=pltpu.CompilerParams(vmem_limit_bytes=VM * MIB),
        cost_estimate=pl.CostEstimate(
            flops=cost * shape[0] * shape[1] * shape[1] * shape[2] * 4,
            bytes_accessed=6 * MIB,
            transcendentals=0,
        ),
    )(at, *amps, *ints)


def add_kernel(fock_ref, mine_ref, sent_ref, out_ref, done, sems):
    rows = out_ref.shape[1] // CHUNKS
    copies = []
    for i in range(CHUNKS):
        at = pl.ds(i * rows, rows)
        cycle = (mine_ref[:, at, :] + sent_ref[:, at, :].astype(jnp.float32)).astype(jnp.bfloat16)
        done[:, at, :] = (fock_ref[:, at, :] + cycle.astype(jnp.float32)).astype(jnp.bfloat16)
        copies.append(pltpu.make_async_copy(done.at[:, at, :], out_ref.at[:, at, :], sems.at[i]))
        copies[-1].start()
    for copy in copies:
        copy.wait()


def add(fock_part, mine, sent):
    return pl.pallas_call(
        add_kernel,
        out_shape=jax.ShapeDtypeStruct(sent.shape, jnp.bfloat16),
        in_specs=[VMEM] * 3,
        out_specs=pl.BlockSpec(memory_space=pl.ANY),
        scratch_shapes=[pltpu.VMEM(sent.shape, jnp.bfloat16), pltpu.SemaphoreType.DMA((CHUNKS,))],
        compiler_params=pltpu.CompilerParams(vmem_limit_bytes=VM * MIB),
    )(fock_part, mine, sent)


def prepare_kernel(at_ref, mask_ref, ints_ref, out_ref):
    occ, depth, n_j, cols = ints_ref.shape
    block = n_j * NZ * NY * depth // n_j // mask_ref.shape[0]
    amp, q = at_ref[0] * NZ + at_ref[1], 2 * at_ref[2] + at_ref[3]
    place = lax.broadcasted_iota(jnp.int32, (depth, cols), 1) // block
    keep = jnp.zeros((depth, cols), jnp.float32)
    for b in range(cols // block):
        present = mask_ref[amp * depth // block, q * (cols // block) + b].astype(jnp.float32)
        keep = jnp.where(place == b, present, keep)
    keep = keep.astype(jnp.bfloat16)
    for k in range(occ):
        for j in range(2):
            pair = [ints_ref[k, :, 2 * j + p, :] * keep for p in range(2)]
            pair = jnp.concatenate(pair, axis=1)
            to = lax.rem(at_ref[1] + k // 2, 2)
            out_ref[to, int(j == k // 2), k % 2] = pair


def prepare(at, tile_mask, cycle_ints):
    occ, depth, _, cols = cycle_ints.shape
    shape = (2, 2, occ // 2, depth, 2 * cols)
    return pl.pallas_call(
        prepare_kernel,
        out_shape=jax.ShapeDtypeStruct(shape, jnp.bfloat16),
        grid_spec=pltpu.PrefetchScalarGridSpec(
            num_scalar_prefetch=2,
            grid=(1,),
            in_specs=[pl.BlockSpec(cycle_ints.shape, lambda r, at, mask: (0, 0, 0, 0))],
            out_specs=pl.BlockSpec(shape, lambda r, at, mask: (0, 0, 0, 0, 0)),
        ),
        compiler_params=pltpu.CompilerParams(vmem_limit_bytes=16 * MIB),
    )(at, tile_mask, cycle_ints)


def swap(a):
    return lax.ppermute(a, "ints", CORES)


def pair_along_z(halves, z):
    got = lax.ppermute(halves[1], "amp", Z_PAIR)
    first = jnp.where(z % 2 == 0, halves[0], got)
    second = jnp.where(z % 2 == 0, got, halves[0])
    return jnp.stack([first, second], axis=1)


def along_z(pair):
    parts = [pair] + [lax.ppermute(pair, "amp", Z_RING(-2 * g)) for g in (1, 2, 3)]
    return [jnp.concatenate([part[r] for part in parts], axis=0) for r in range(2)]


def spread(a, axis, groups):
    a = jnp.broadcast_to(a[None], (len(groups[0]),) + a.shape)
    return lax.all_to_all(a, axis, 0, 0, axis_index_groups=groups)


def along_y(row):
    return [row] + [lax.ppermute(row, "amp", Y_RING(-e)) for e in (1, 2, 3)]


def body(amplitudes, fock_vv, cycle_ints, tile_mask):
    amp, ints = lax.axis_index("amp"), lax.axis_index("ints")
    at = jnp.stack([amp // NZ, amp % NZ, ints // 2, ints % 2]).astype(jnp.int32)
    halves = prepare(at, tile_mask, cycle_ints)
    rows = along_z(pair_along_z(halves, at[1]))
    gathered = spread(amplitudes, "ints", X_GROUPS)
    gathered, *rows = lax.optimization_barrier((gathered, *rows))
    partners, mine = along_y(rows[0]), along_y(rows[1])
    own = [gathered, swap(gathered)]

    fock_rows = lax.dynamic_slice_in_dim(fock_vv, ints * amplitudes.shape[2], amplitudes.shape[2], 0)
    fock_part = fock_terms(at, fock_vv, fock_rows, [amplitudes, *own])
    sent = cycle_sum(at, own, partners, jnp.bfloat16, COST)
    sent = lax.ppermute(sent, "amp", Z_PAIR)
    return add(fock_part, cycle_sum(at, own, mine, jnp.float32, MINE_COST), sent)


def solution(mesh):
    in_specs = (P("amp", None, "ints"), P(), P(None, "amp", None, "ints"), P())
    out_specs = P("amp", None, "ints")
    return jax.shard_map(body, mesh=mesh, in_specs=in_specs, out_specs=out_specs, check_vma=False)
```

```python
import functools

import jax
import jax.numpy as jnp
from jax import lax
from jax.experimental import pallas as pl
from jax.experimental.pallas import tpu as pltpu
from jax.sharding import PartitionSpec as P

NX, NY, NZ = 4, 4, 8
X_RING = lambda d: [(2 * x + c, 2 * ((x + d) % NX) + c) for x in range(NX) for c in range(2)]
Y_RING = lambda d: [(y * NZ + z, ((y + d) % NY) * NZ + z) for y in range(NY) for z in range(NZ)]
Z_PAIR = [(p, p ^ 1) for p in range(NY * NZ)]
CORES = [(q, q ^ 1) for q in range(2 * NX)]
X_GROUPS = [[2 * x + c for x in range(NX)] for c in range(2)]
Y_GROUPS = [[y * NZ + z for y in range(NY)] for z in range(NZ)]
Z_RING = lambda d: [(y * NZ + z, y * NZ + (z + d) % NZ) for y in range(NY) for z in range(NZ)]
ROWS = 256
MIB = 1 << 20


VM = 16
COST = 8
CROWS = 512
CHUNKS = 4
MINE_COST = 8


VMEM = pl.BlockSpec(memory_space=pltpu.VMEM)
SMEM = pl.BlockSpec(memory_space=pltpu.SMEM)


def blocks_of(refs):
    return [ref.at[d] for d in range(NX) for ref in refs]


def fock_kernel(at_ref, fock_ref, rows_ref, *refs):
    amps, out_ref = refs[:-1], refs[-1]
    x, core = 0, at_ref[3]
    own, amps = amps[0], blocks_of(amps[1:])
    width = own.shape[2]
    both = jnp.concatenate([own[0], own[1]], axis=1)
    fock = []
    for i in range(len(amps)):
        chip, c = lax.rem(x + i // 2, NX), (1 - core if i % 2 else core)
        start = pl.multiple_of((2 * chip + c) * width, width)
        fock.append(rows_ref[:, pl.ds(start, width)])
    fock = jnp.concatenate(fock, axis=1)

    @pl.loop(0, fock_ref.shape[0] // ROWS)
    def _(r):
        at = pl.ds(pl.multiple_of(r * ROWS, ROWS), ROWS)
        left = jnp.dot(fock_ref[at, :], both, preferred_element_type=jnp.float32)
        for p in range(2):
            rows = jnp.concatenate([a[p, at, :] for a in amps], axis=1)
            right = lax.dot_general(
                rows, fock, (((1,), (1,)), ((), ())), preferred_element_type=jnp.float32
            )
            out_ref[p, at, :] = left[:, p * width : (p + 1) * width] + right


def fock_terms(at, fock_vv, fock_rows, amps):
    pairs, width, cols = amps[0].shape
    return pl.pallas_call(
        fock_kernel,
        out_shape=jax.ShapeDtypeStruct((pairs, width, cols), jnp.float32),
        in_specs=[SMEM] + [VMEM] * (2 + len(amps)),
        out_specs=VMEM,
        compiler_params=pltpu.CompilerParams(vmem_limit_bytes=VM * MIB),
        cost_estimate=pl.CostEstimate(
            flops=1 * 4 * pairs * width * width * cols, bytes_accessed=4 * MIB, transcendentals=0
        ),
    )(at, fock_vv, fock_rows, *amps)


def cycle_kernel(first, at_ref, *refs):
    held, out_ref, refs = refs[-1], refs[-2], refs[:-2]
    ints, amps = refs[-NY:], refs[:-NY]
    y, z, core = at_ref[0], at_ref[1], at_ref[3]
    amps = blocks_of(amps)
    n_z, pairs, depth, cols = ints[0].shape
    width = cols // 2
    for e in range(NY):
        chip = lax.rem(y + e, NY)
        for g in range(n_z // 2):
            place = lax.rem(z // 2 + g, n_z // 2)
            s = lax.rem(place // 2 + core, 2)
            for p in range(pairs):
                part = ints[e][2 * g : 2 * g + 2, p]
                held[chip, s, p, lax.rem(place, 2)] = part.reshape(2 * depth, cols)
    rhs = jnp.concatenate(
        [held[i // 2, i % 2, p].reshape(n_z // 2 * depth, cols) for p in range(pairs) for i in range(len(amps))], axis=0
    )

    @pl.loop(0, out_ref.shape[1] // CROWS)
    def _(r):
        to = pl.ds(pl.multiple_of(r * CROWS, CROWS), CROWS)
        at = pl.ds(pl.multiple_of(first + r * CROWS, CROWS), CROWS)
        lhs = jnp.concatenate([a[p, at, :] for p in range(pairs) for a in amps], axis=1)
        total = jnp.dot(lhs, rhs, preferred_element_type=jnp.float32)
        for p in range(pairs):
            out_ref[p, to, :] = total[:, p * width : (p + 1) * width].astype(out_ref.dtype)


def cycle_sum(at, amps, ints, dtype, cost, first, rows):
    n_z, pairs, depth, cols = ints[0].shape
    shape = (pairs, rows, amps[0].shape[-1])
    return pl.pallas_call(
        functools.partial(cycle_kernel, first),
        out_shape=jax.ShapeDtypeStruct(shape, dtype),
        in_specs=[SMEM] + [VMEM] * (len(amps) + len(ints)),
        out_specs=VMEM,
        scratch_shapes=[pltpu.VMEM((NY, 2, pairs, 2, 2 * depth, cols), jnp.bfloat16)],
        compiler_params=pltpu.CompilerParams(vmem_limit_bytes=VM * MIB),
        cost_estimate=pl.CostEstimate(
            flops=cost * pairs * rows * 8 * rows * cols,
            bytes_accessed=6 * MIB,
            transcendentals=0,
        ),
    )(at, *amps, *ints)


def add_kernel(fock_ref, mine_ref, low_ref, high_ref, out_ref, done, sems):
    rows = out_ref.shape[1] // CHUNKS
    copies = []
    for i in range(CHUNKS):
        at = pl.ds(i * rows, rows)
        sent_ref, part = (low_ref, i) if i < CHUNKS // 2 else (high_ref, i - CHUNKS // 2)
        sent = sent_ref[:, pl.ds(part * rows, rows), :].astype(jnp.float32)
        cycle = (mine_ref[:, at, :] + sent).astype(jnp.bfloat16)
        done[:, at, :] = (fock_ref[:, at, :] + cycle.astype(jnp.float32)).astype(jnp.bfloat16)
        copies.append(pltpu.make_async_copy(done.at[:, at, :], out_ref.at[:, at, :], sems.at[i]))
        copies[-1].start()
    for copy in copies:
        copy.wait()


def add(fock_part, mine, low, high):
    return pl.pallas_call(
        add_kernel,
        out_shape=jax.ShapeDtypeStruct(mine.shape, jnp.bfloat16),
        in_specs=[VMEM] * 4,
        out_specs=pl.BlockSpec(memory_space=pl.ANY),
        scratch_shapes=[pltpu.VMEM(mine.shape, jnp.bfloat16), pltpu.SemaphoreType.DMA((CHUNKS,))],
        compiler_params=pltpu.CompilerParams(vmem_limit_bytes=VM * MIB),
    )(fock_part, mine, low, high)


def prepare_kernel(at_ref, mask_ref, ints_ref, out_ref):
    occ, depth, n_j, cols = ints_ref.shape
    block = n_j * NZ * NY * depth // n_j // mask_ref.shape[0]
    amp, q = at_ref[0] * NZ + at_ref[1], 2 * at_ref[2] + at_ref[3]
    place = lax.broadcasted_iota(jnp.int32, (depth, cols), 1) // block
    keep = jnp.zeros((depth, cols), jnp.float32)
    for b in range(cols // block):
        present = mask_ref[amp * depth // block, q * (cols // block) + b].astype(jnp.float32)
        keep = jnp.where(place == b, present, keep)
    keep = keep.astype(jnp.bfloat16)
    for k in range(occ):
        for j in range(2):
            pair = [ints_ref[k, :, 2 * j + p, :] * keep for p in range(2)]
            pair = jnp.concatenate(pair, axis=1)
            to = lax.rem(at_ref[1] + k // 2, 2)
            out_ref[to, int(j == k // 2), k % 2] = pair


def prepare(at, tile_mask, cycle_ints):
    occ, depth, _, cols = cycle_ints.shape
    shape = (2, 2, occ // 2, depth, 2 * cols)
    return pl.pallas_call(
        prepare_kernel,
        out_shape=jax.ShapeDtypeStruct(shape, jnp.bfloat16),
        grid_spec=pltpu.PrefetchScalarGridSpec(
            num_scalar_prefetch=2,
            grid=(1,),
            in_specs=[pl.BlockSpec(cycle_ints.shape, lambda r, at, mask: (0, 0, 0, 0))],
            out_specs=pl.BlockSpec(shape, lambda r, at, mask: (0, 0, 0, 0, 0)),
        ),
        compiler_params=pltpu.CompilerParams(vmem_limit_bytes=16 * MIB),
    )(at, tile_mask, cycle_ints)


def swap(a):
    return lax.ppermute(a, "ints", CORES)


def pair_along_z(halves, z):
    got = lax.ppermute(halves[1], "amp", Z_PAIR)
    first = jnp.where(z % 2 == 0, halves[0], got)
    second = jnp.where(z % 2 == 0, got, halves[0])
    return jnp.stack([first, second], axis=1)


def along_z(pair):
    parts = [pair] + [lax.ppermute(pair, "amp", Z_RING(-2 * g)) for g in (1, 2, 3)]
    return [jnp.concatenate([part[r] for part in parts], axis=0) for r in range(2)]


def spread(a, axis, groups):
    a = jnp.broadcast_to(a[None], (len(groups[0]),) + a.shape)
    return lax.all_to_all(a, axis, 0, 0, axis_index_groups=groups)


def along_y(row):
    return [row] + [lax.ppermute(row, "amp", Y_RING(-e)) for e in (1, 2, 3)]


def body(amplitudes, fock_vv, cycle_ints, tile_mask):
    amp, ints = lax.axis_index("amp"), lax.axis_index("ints")
    at = jnp.stack([amp // NZ, amp % NZ, ints // 2, ints % 2]).astype(jnp.int32)
    halves = prepare(at, tile_mask, cycle_ints)
    rows = along_z(pair_along_z(halves, at[1]))
    gathered = spread(amplitudes, "ints", X_GROUPS)
    gathered, *rows = lax.optimization_barrier((gathered, *rows))
    partners = along_y(rows[0])
    second, _ = lax.optimization_barrier((rows[1], partners[2]))
    mine = along_y(second)
    own = [gathered, swap(gathered)]

    fock_rows = lax.dynamic_slice_in_dim(fock_vv, ints * amplitudes.shape[2], amplitudes.shape[2], 0)
    fock_part = fock_terms(at, fock_vv, fock_rows, [amplitudes, *own])
    rows = amplitudes.shape[1]
    sent = []
    for first in range(0, rows, rows // 2):
        half = cycle_sum(at, own, partners, jnp.bfloat16, COST, first, rows // 2)
        sent.append(lax.ppermute(half, "amp", Z_PAIR))
    mine[0], _ = lax.optimization_barrier((mine[0], fock_part))
    mine = cycle_sum(at, own, mine, jnp.float32, MINE_COST, 0, rows)
    return add(fock_part, mine, *sent)


def solution(mesh):
    in_specs = (P("amp", None, "ints"), P(), P(None, "amp", None, "ints"), P())
    out_specs = P("amp", None, "ints")
    return jax.shard_map(body, mesh=mesh, in_specs=in_specs, out_specs=out_specs, check_vma=False)
```

```python
import functools

import jax
import jax.numpy as jnp
from jax import lax
from jax.experimental import pallas as pl
from jax.experimental.pallas import tpu as pltpu
from jax.sharding import PartitionSpec as P

NX, NY, NZ = 4, 4, 8
X_RING = lambda d: [(2 * x + c, 2 * ((x + d) % NX) + c) for x in range(NX) for c in range(2)]
Y_RING = lambda d: [(y * NZ + z, ((y + d) % NY) * NZ + z) for y in range(NY) for z in range(NZ)]
Z_PAIR = [(p, p ^ 1) for p in range(NY * NZ)]
CORES = [(q, q ^ 1) for q in range(2 * NX)]
X_GROUPS = [[2 * x + c for x in range(NX)] for c in range(2)]
Y_GROUPS = [[y * NZ + z for y in range(NY)] for z in range(NZ)]
Z_RING = lambda d: [(y * NZ + z, y * NZ + (z + d) % NZ) for y in range(NY) for z in range(NZ)]
ROWS = 256
MIB = 1 << 20


VM = 16
COST = 8
CROWS = 512
CHUNKS = 4
MINE_COST = 8


VMEM = pl.BlockSpec(memory_space=pltpu.VMEM)
SMEM = pl.BlockSpec(memory_space=pltpu.SMEM)


def blocks_of(refs):
    return [ref.at[d] for d in range(NX) for ref in refs]


def fock_kernel(at_ref, fock_ref, rows_ref, *refs):
    amps, out_ref = refs[:-1], refs[-1]
    x, core = 0, at_ref[3]
    own, amps = amps[0], blocks_of(amps[1:])
    width = own.shape[2]
    both = jnp.concatenate([own[0], own[1]], axis=1)
    fock = []
    for i in range(len(amps)):
        chip, c = lax.rem(x + i // 2, NX), (1 - core if i % 2 else core)
        start = pl.multiple_of((2 * chip + c) * width, width)
        fock.append(rows_ref[:, pl.ds(start, width)])
    fock = jnp.concatenate(fock, axis=1)

    @pl.loop(0, fock_ref.shape[0] // ROWS)
    def _(r):
        at = pl.ds(pl.multiple_of(r * ROWS, ROWS), ROWS)
        left = jnp.dot(fock_ref[at, :], both, preferred_element_type=jnp.float32)
        for p in range(2):
            rows = jnp.concatenate([a[p, at, :] for a in amps], axis=1)
            right = lax.dot_general(
                rows, fock, (((1,), (1,)), ((), ())), preferred_element_type=jnp.float32
            )
            out_ref[p, at, :] = left[:, p * width : (p + 1) * width] + right


def fock_terms(at, fock_vv, fock_rows, amps):
    pairs, width, cols = amps[0].shape
    return pl.pallas_call(
        fock_kernel,
        out_shape=jax.ShapeDtypeStruct((pairs, width, cols), jnp.float32),
        in_specs=[SMEM] + [VMEM] * (2 + len(amps)),
        out_specs=VMEM,
        compiler_params=pltpu.CompilerParams(vmem_limit_bytes=VM * MIB),
        cost_estimate=pl.CostEstimate(
            flops=1 * 4 * pairs * width * width * cols, bytes_accessed=4 * MIB, transcendentals=0
        ),
    )(at, fock_vv, fock_rows, *amps)


def cycle_kernel(first, at_ref, *refs):
    held, out_ref, refs = refs[-1], refs[-2], refs[:-2]
    ints, amps = refs[-NY:], refs[:-NY]
    y, z, core = at_ref[0], at_ref[1], at_ref[3]
    amps = blocks_of(amps)
    n_z, pairs, depth, cols = ints[0].shape
    width = cols // 2
    for e in range(NY):
        chip = lax.rem(y + e, NY)
        for g in range(n_z // 2):
            place = lax.rem(z // 2 + g, n_z // 2)
            s = lax.rem(place // 2 + core, 2)
            for p in range(pairs):
                part = ints[e][2 * g : 2 * g + 2, p]
                held[chip, s, p, lax.rem(place, 2)] = part.reshape(2 * depth, cols)
    rhs = jnp.concatenate(
        [held[i // 2, i % 2, p].reshape(n_z // 2 * depth, cols) for p in range(pairs) for i in range(len(amps))], axis=0
    )

    @pl.loop(0, out_ref.shape[1] // CROWS)
    def _(r):
        to = pl.ds(pl.multiple_of(r * CROWS, CROWS), CROWS)
        at = pl.ds(pl.multiple_of(first + r * CROWS, CROWS), CROWS)
        lhs = jnp.concatenate([a[p, at, :] for p in range(pairs) for a in amps], axis=1)
        total = jnp.dot(lhs, rhs, preferred_element_type=jnp.float32)
        for p in range(pairs):
            out_ref[p, to, :] = total[:, p * width : (p + 1) * width].astype(out_ref.dtype)


def cycle_sum(at, amps, ints, dtype, cost, first, rows):
    n_z, pairs, depth, cols = ints[0].shape
    shape = (pairs, rows, amps[0].shape[-1])
    return pl.pallas_call(
        functools.partial(cycle_kernel, first),
        out_shape=jax.ShapeDtypeStruct(shape, dtype),
        in_specs=[SMEM] + [VMEM] * (len(amps) + len(ints)),
        out_specs=VMEM,
        scratch_shapes=[pltpu.VMEM((NY, 2, pairs, 2, 2 * depth, cols), jnp.bfloat16)],
        compiler_params=pltpu.CompilerParams(vmem_limit_bytes=VM * MIB),
        cost_estimate=pl.CostEstimate(
            flops=cost * pairs * rows * 8 * rows * cols,
            bytes_accessed=6 * MIB,
            transcendentals=0,
        ),
    )(at, *amps, *ints)


def add_kernel(fock_ref, mine_ref, low_ref, high_ref, out_ref, done, sems):
    rows = out_ref.shape[1] // CHUNKS
    copies = []
    for i in range(CHUNKS):
        at = pl.ds(i * rows, rows)
        sent_ref, part = (low_ref, i) if i < CHUNKS // 2 else (high_ref, i - CHUNKS // 2)
        sent = sent_ref[:, pl.ds(part * rows, rows), :].astype(jnp.float32)
        cycle = (mine_ref[:, at, :] + sent).astype(jnp.bfloat16)
        done[:, at, :] = (fock_ref[:, at, :] + cycle.astype(jnp.float32)).astype(jnp.bfloat16)
        copies.append(pltpu.make_async_copy(done.at[:, at, :], out_ref.at[:, at, :], sems.at[i]))
        copies[-1].start()
    for copy in copies:
        copy.wait()


def add(fock_part, mine, low, high):
    return pl.pallas_call(
        add_kernel,
        out_shape=jax.ShapeDtypeStruct(mine.shape, jnp.bfloat16),
        in_specs=[VMEM] * 4,
        out_specs=pl.BlockSpec(memory_space=pl.ANY),
        scratch_shapes=[pltpu.VMEM(mine.shape, jnp.bfloat16), pltpu.SemaphoreType.DMA((CHUNKS,))],
        compiler_params=pltpu.CompilerParams(vmem_limit_bytes=VM * MIB),
    )(fock_part, mine, low, high)


def prepare_kernel(at_ref, mask_ref, ints_ref, out_ref):
    occ, depth, n_j, cols = ints_ref.shape
    block = n_j * NZ * NY * depth // n_j // mask_ref.shape[0]
    amp, q = at_ref[0] * NZ + at_ref[1], 2 * at_ref[2] + at_ref[3]
    place = lax.broadcasted_iota(jnp.int32, (depth, cols), 1) // block
    keep = jnp.zeros((depth, cols), jnp.float32)
    for b in range(cols // block):
        present = mask_ref[amp * depth // block, q * (cols // block) + b].astype(jnp.float32)
        keep = jnp.where(place == b, present, keep)
    keep = keep.astype(jnp.bfloat16)
    for k in range(occ):
        for j in range(2):
            pair = [ints_ref[k, :, 2 * j + p, :] * keep for p in range(2)]
            pair = jnp.concatenate(pair, axis=1)
            to = lax.rem(at_ref[1] + k // 2, 2)
            out_ref[to, int(j == k // 2), k % 2] = pair


def prepare(at, tile_mask, cycle_ints):
    occ, depth, _, cols = cycle_ints.shape
    shape = (2, 2, occ // 2, depth, 2 * cols)
    return pl.pallas_call(
        prepare_kernel,
        out_shape=jax.ShapeDtypeStruct(shape, jnp.bfloat16),
        grid_spec=pltpu.PrefetchScalarGridSpec(
            num_scalar_prefetch=2,
            grid=(1,),
            in_specs=[pl.BlockSpec(cycle_ints.shape, lambda r, at, mask: (0, 0, 0, 0))],
            out_specs=pl.BlockSpec(shape, lambda r, at, mask: (0, 0, 0, 0, 0)),
        ),
        compiler_params=pltpu.CompilerParams(vmem_limit_bytes=16 * MIB),
    )(at, tile_mask, cycle_ints)


def swap(a):
    return lax.ppermute(a, "ints", CORES)


def pair_along_z(halves, z):
    got = lax.ppermute(halves[1], "amp", Z_PAIR)
    first = jnp.where(z % 2 == 0, halves[0], got)
    second = jnp.where(z % 2 == 0, got, halves[0])
    return jnp.stack([first, second], axis=1)


def along_z(pair):
    parts = [pair] + [lax.ppermute(pair, "amp", Z_RING(-2 * g)) for g in (1, 2, 3)]
    return [jnp.concatenate([part[r] for part in parts], axis=0) for r in range(2)]


def spread(a, axis, groups):
    a = jnp.broadcast_to(a[None], (len(groups[0]),) + a.shape)
    return lax.all_to_all(a, axis, 0, 0, axis_index_groups=groups)


def along_y(row):
    return [row] + [lax.ppermute(row, "amp", Y_RING(-e)) for e in (1, 2, 3)]


def body(amplitudes, fock_vv, cycle_ints, tile_mask):
    amp, ints = lax.axis_index("amp"), lax.axis_index("ints")
    at = jnp.stack([amp // NZ, amp % NZ, ints // 2, ints % 2]).astype(jnp.int32)
    fock_rows = lax.dynamic_slice_in_dim(fock_vv, ints * amplitudes.shape[2], amplitudes.shape[2], 0)
    halves = prepare(at, tile_mask, cycle_ints)
    halves, fock_rows = lax.optimization_barrier((halves, fock_rows))
    rows = along_z(pair_along_z(halves, at[1]))
    gathered = spread(amplitudes, "ints", X_GROUPS)
    gathered, *rows = lax.optimization_barrier((gathered, *rows))
    partners = along_y(rows[0])
    second, _ = lax.optimization_barrier((rows[1], partners[2]))
    mine = along_y(second)
    own = [gathered, swap(gathered)]

    fock_part = fock_terms(at, fock_vv, fock_rows, [amplitudes, *own])
    rows = amplitudes.shape[1]
    sent = []
    for first in range(0, rows, rows // 2):
        half = cycle_sum(at, own, partners, jnp.bfloat16, COST, first, rows // 2)
        sent.append(lax.ppermute(half, "amp", Z_PAIR))
    mine[0], _ = lax.optimization_barrier((mine[0], fock_part))
    mine = cycle_sum(at, own, mine, jnp.float32, MINE_COST, 0, rows)
    return add(fock_part, mine, *sent)


def solution(mesh):
    in_specs = (P("amp", None, "ints"), P(), P(None, "amp", None, "ints"), P())
    out_specs = P("amp", None, "ints")
    return jax.shard_map(body, mesh=mesh, in_specs=in_specs, out_specs=out_specs, check_vma=False)
```
